32 devices in a mesh: groups: 2 (over y), fsdp: 4 (over z), tensor: 4 (over x, core).
Axes of the slice: x: 2, y: 2, z: 4, core: 2. Of those that a mesh axis runs over, the one named last changes fastest.
Arguments:
- layer_input_rows: bfloat16 [4, 16, 8192], P(None, ('groups', 'fsdp')), parts along dimension 1, may hold values from -6 to 6
- prenorm_scale: bfloat16 [8192], replicated, may hold values from 0.5 to 1.5
- query_key_value_weight: bfloat16 [8192, 8, 1280], P('fsdp', 'tensor'), may hold values from -0.0625 to 0.0625
- output_weight: bfloat16 [8, 1024, 8192], P('tensor', None, 'fsdp'), may hold values from -0.0625 to 0.0625
- query_down_factor: bfloat16 [64, 8192], P('fsdp'), may hold values from -0.0625 to 0.0625
- query_up_factor: bfloat16 [8, 64, 1024], P('tensor', 'fsdp'), may hold values from -0.29882812 to 0.29882812
- output_down_factor: bfloat16 [8, 64, 1024], P('tensor', 'fsdp'), may hold values from -0.0625 to 0.0625
- output_up_factor: bfloat16 [64, 8192], P('fsdp'), may hold values from -0.29882812 to 0.29882812
- stored_keys: bfloat16 [16, 8, 2048, 128], P(('groups', 'fsdp'), 'tensor'), parts along dimension 0, may hold values from -68 to 68
- stored_values: bfloat16 [16, 8, 2048, 128], P(('groups', 'fsdp'), 'tensor'), parts along dimension 0, may hold values from -6 to 6
- lengths: int32 [16], P(('groups', 'fsdp')), parts along dimension 0, may hold values from 1 to 2048, as said below
Outputs:
- hidden_out: bfloat16 [4, 16, 8192], P(None, ('groups', 'fsdp')), parts along dimension 1
The draws below stay inside these ranges and needn't reach their ends.
There are 2 independent parts, one for each index of `groups`. The reference program is written for one: setup_inputs(seed, part) draws one part's arguments, and reference() takes and returns one part's arrays. A program takes and returns all parts, laid end to end along the dimension named above; an argument that names none is the same for every part. Nothing has to cross between parts.
Inputs may be any that keep to these rules, and one draw needn't show every extreme that they name: `lengths`: some row has exactly 2048 live positions in every draw.
All inputs are finite; a program needn't handle non-finite values.
Results may differ from the reference program's by a relative error of at most 0.013.
The reference program's roundings to bfloat16 on the way count: a program that leaves them out, or rounds other values in their place, can miss the bound.
Values may be sent and summed in bfloat16 or wider, within the bound.
No kernel may reach another device: no remote copies, remote signals or barrier semaphores. Data moves between devices by JAX's collectives and lax.ppermute only.
A program may use at most 128 MiB of HBM per device.

```python
import jax
import jax.numpy as jnp
from jax import lax

MODEL_WIDTH = 8192
QUERY_HEADS = 64
KEY_VALUE_HEADS = 8
HEAD_SIZE = 128
ADAPTER_RANK = 64
STEPS = 4
CACHE = 2048
ROWS = 8


def draw_stored_keys(key, part):
    key = jax.random.fold_in(key, 11)
    key_draw = jax.random.fold_in(key, 0)
    shape = (ROWS, KEY_VALUE_HEADS, CACHE, HEAD_SIZE)
    base = jnp.clip(jax.random.normal(key_draw, shape, jnp.float32), -6.0, 6.0)
    return base.astype(jnp.bfloat16)


def draw_lengths(key, part):
    key = jax.random.fold_in(key, 5)
    key_draw, key_pick = jax.random.split(key)
    drawn = jax.random.randint(key_draw, (ROWS,), 1, CACHE + 1)
    longest = jax.random.randint(key_pick, (), 0, ROWS)
    return jnp.where(jnp.arange(ROWS) == longest, CACHE, drawn).astype(jnp.int32)


def levels(key, shape, cuts, low, high):
    def one(position, shards_of):
        heights = jax.random.uniform(jax.random.fold_in(jax.random.fold_in(key, 6), position), (shards_of,), jnp.float32, low / len(cuts), high / len(cuts))
        return jnp.repeat(jnp.exp(heights), shape[position] // shards_of).reshape((-1,) + (1,) * (len(shape) - position - 1))

    level = one(*cuts[0])
    for cut in cuts[1:]:
        level = level * one(*cut)
    return level


def gaussian(rng, dims, width, most, cuts=(), kind=jnp.bfloat16):
    values = jax.random.normal(rng, dims, jnp.float32) * width
    if len(cuts) > 0:
        values = levels(rng, dims, cuts, -0.22, 0.18) * values
    return jnp.clip(values, min=-most, max=most).astype(kind)


def setup_inputs(seed: int = 0, part: int = 0) -> dict:
    keys = jax.random.split(jax.random.key(seed), 12)
    part_keys = jax.random.split(jax.random.fold_in(keys[11], part), 12)
    layer_input_rows = gaussian(part_keys[0], (STEPS, ROWS, MODEL_WIDTH), 1.0, 6.0, ((1, 4),))
    prenorm_scale = jnp.clip(1.0 + 0.1 * jax.random.normal(keys[1], (MODEL_WIDTH,), jnp.float32), 0.5, 1.5).astype(jnp.bfloat16)
    query_key_value_weight = gaussian(keys[2], (MODEL_WIDTH, KEY_VALUE_HEADS, (QUERY_HEADS // KEY_VALUE_HEADS + 2) * HEAD_SIZE), MODEL_WIDTH ** -0.5, 0.0625, ((0, 4), (1, 4)))
    output_weight = gaussian(keys[3], (KEY_VALUE_HEADS, (QUERY_HEADS // KEY_VALUE_HEADS) * HEAD_SIZE, MODEL_WIDTH), (QUERY_HEADS * HEAD_SIZE) ** -0.5, 0.0625, ((0, 4), (2, 4)))
    query_down_factor = gaussian(keys[4], (ADAPTER_RANK, MODEL_WIDTH), MODEL_WIDTH ** -0.5, 0.0625, ((0, 4),))
    query_up_factor = gaussian(keys[5], (KEY_VALUE_HEADS, ADAPTER_RANK, (QUERY_HEADS // KEY_VALUE_HEADS) * HEAD_SIZE), 0.05, 0.29882812, ((0, 4), (1, 4)))
    output_down_factor = gaussian(keys[6], (KEY_VALUE_HEADS, ADAPTER_RANK, (QUERY_HEADS // KEY_VALUE_HEADS) * HEAD_SIZE), (QUERY_HEADS * HEAD_SIZE) ** -0.5, 0.0625, ((0, 4), (1, 4)))
    output_up_factor = gaussian(keys[7], (ADAPTER_RANK, MODEL_WIDTH), 0.05, 0.29882812, ((0, 4),))
    stored_keys = draw_stored_keys(jax.random.fold_in(jax.random.fold_in(keys[11], part), 71), part)
    stored_values = gaussian(part_keys[9], (ROWS, KEY_VALUE_HEADS, CACHE, HEAD_SIZE), 1.0, 6.0, ((0, 4), (1, 4)))
    lengths = draw_lengths(jax.random.fold_in(jax.random.fold_in(keys[11], part), 71), part)
    return {"layer_input_rows": layer_input_rows, "prenorm_scale": prenorm_scale, "query_key_value_weight": query_key_value_weight, "output_weight": output_weight, "query_down_factor": query_down_factor, "query_up_factor": query_up_factor, "output_down_factor": output_down_factor, "output_up_factor": output_up_factor, "stored_keys": stored_keys, "stored_values": stored_values, "lengths": lengths}


EPS = 1e-05
ADAPTER_SCALE = 2.0

def reference(layer_input_rows, prenorm_scale, query_key_value_weight, output_weight, query_down_factor, query_up_factor, output_down_factor, output_up_factor, stored_keys, stored_values, lengths):
    q_per_kv = QUERY_HEADS // KEY_VALUE_HEADS
    query_width = q_per_kv * HEAD_SIZE
    query_update = ADAPTER_SCALE * jnp.einsum('xu,gxw->ugw', query_down_factor.astype(jnp.float32), query_up_factor.astype(jnp.float32))
    combined_query_weight = (query_key_value_weight[:, :, :query_width].astype(jnp.float32) + query_update).astype(jnp.bfloat16)
    merged_qkv = jnp.concatenate([combined_query_weight, query_key_value_weight[:, :, query_width:]], axis=2)
    output_update = ADAPTER_SCALE * jnp.einsum('xts,tz->xsz', output_down_factor.astype(jnp.float32), output_up_factor.astype(jnp.float32))
    combined_output_weight = (output_weight.astype(jnp.float32) + output_update).astype(jnp.bfloat16)
    flat_qkv = merged_qkv.reshape(MODEL_WIDTH, KEY_VALUE_HEADS * (q_per_kv + 2) * HEAD_SIZE)
    flat_out = combined_output_weight.reshape(KEY_VALUE_HEADS * query_width, MODEL_WIDTH)
    keys_float = stored_keys.astype(jnp.float32)
    values_float = stored_values.astype(jnp.float32)
    positions = jnp.arange(CACHE, dtype=jnp.int32)
    valid = positions[None, :] < lengths[:, None]
    score_scale = 1.0 / HEAD_SIZE ** 0.5
    window_keys = []
    window_values = []
    results = []
    for window_step in range(STEPS):
        tok_rows = layer_input_rows[window_step].astype(jnp.float32)
        spread_sq = lax.optimization_barrier(jnp.mean(tok_rows * tok_rows, axis=-1, keepdims=True))
        normed = (tok_rows * lax.rsqrt(spread_sq + EPS) * prenorm_scale.astype(jnp.float32)).astype(jnp.bfloat16)
        projected = jnp.dot(normed, flat_qkv, preferred_element_type=jnp.float32).astype(jnp.bfloat16)
        projected = projected.reshape(ROWS, KEY_VALUE_HEADS, q_per_kv + 2, HEAD_SIZE)
        query = projected[:, :, :q_per_kv].astype(jnp.float32)
        window_keys.append(projected[:, :, q_per_kv])
        window_values.append(projected[:, :, q_per_kv + 1])
        win_keys = jnp.stack(window_keys, 2).astype(jnp.float32)
        win_values = jnp.stack(window_values, 2).astype(jnp.float32)
        score_cache = jnp.einsum('rkgh,rklh->rkgl', query, keys_float) * score_scale
        score_cache = jnp.where(valid[:, None, None, :], score_cache, -1e+30)
        score_win = jnp.einsum('rkgh,rkwh->rkgw', query, win_keys) * score_scale
        peak = jnp.maximum(lax.optimization_barrier(jnp.max(score_cache, axis=-1)), lax.optimization_barrier(jnp.max(score_win, axis=-1)))
        exp_cache = jnp.exp(score_cache - peak[..., None])
        exp_win = jnp.exp(score_win - peak[..., None])
        total = lax.optimization_barrier(jnp.sum(exp_cache, axis=-1)) + lax.optimization_barrier(jnp.sum(exp_win, axis=-1))
        weight_cache = (exp_cache / total[..., None]).astype(jnp.bfloat16).astype(jnp.float32)
        weight_win = (exp_win / total[..., None]).astype(jnp.bfloat16).astype(jnp.float32)
        context = jnp.einsum('rkgl,rklh->rkgh', weight_cache, values_float)
        context = context + jnp.einsum('rkgw,rkwh->rkgh', weight_win, win_values)
        context = context.astype(jnp.bfloat16).reshape(ROWS, KEY_VALUE_HEADS * query_width)
        attended = jnp.dot(context, flat_out, preferred_element_type=jnp.float32)
        results.append((tok_rows + attended).astype(jnp.bfloat16))
    return jnp.stack(results, 0)
```

```python
import functools

import jax
import jax.numpy as jnp
from jax import lax
from jax.experimental import pallas as pl
from jax.experimental.pallas import tpu as pltpu
from jax.sharding import PartitionSpec as P

QUERY_HEADS = 64
KEY_VALUE_HEADS = 8
HEAD_SIZE = 128
EPS = 1e-05
ADAPTER_SCALE = 2.0

GROUP = QUERY_HEADS // KEY_VALUE_HEADS
QUERY_WIDTH = GROUP * HEAD_SIZE
HEAD_WIDTH = QUERY_WIDTH + 2 * HEAD_SIZE
F32 = jnp.float32
BF16 = jnp.bfloat16
MIB = 2**20
VMEM = pl.BlockSpec(memory_space=pltpu.VMEM)
SMEM = pl.BlockSpec(memory_space=pltpu.SMEM)
ANY = pl.BlockSpec(memory_space=pl.ANY)


def params(mib):
    return pltpu.CompilerParams(vmem_limit_bytes=mib * MIB)


def dot(a, b):
    return jnp.dot(a, b, preferred_element_type=F32)


def dot_nt(a, b):
    return lax.dot_general(a, b, (((1,), (1,)), ((), ())), preferred_element_type=F32)


def dot_split(a, b):
    high = a.astype(BF16)
    low = (a - high.astype(F32)).astype(BF16)
    return dot(high, b) + dot(low, b)


def swap(x, axis, mask):
    size = lax.axis_size(axis)
    return lax.ppermute(x, axis, [(i, i ^ mask) for i in range(size)])


def pack_kernel(ranks, parts, index, down, up, *outs):
    heads = down.shape[0]
    width = outs[0].shape[1] - heads * QUERY_WIDTH
    for j in range(parts):
        for k in range(heads):
            outs[j][:, k * QUERY_WIDTH : (k + 1) * QUERY_WIDTH] = down[k]
        start = pl.multiple_of((index[0] ^ j) * width, 128)
        outs[j][:, heads * QUERY_WIDTH :] = up[:, pl.ds(start, width)]


def project_kernel(parts, blocks, index, *refs):
    x = refs[:parts]
    scale, weight, down, up = refs[parts : parts + 4]
    outs = refs[parts + 4 : 2 * parts + 4]
    normed, wide, buf, sems = refs[2 * parts + 4 :]
    span, heads = weight.shape[:2]
    steps, rows, width = x[0].shape
    tokens = steps * rows
    total = parts * tokens
    chunk = span // blocks
    copies = [
        pltpu.make_async_copy(
            weight.at[pl.ds(b * chunk, chunk)], buf.at[pl.ds(b * chunk, chunk)], sems.at[b]
        )
        for b in range(blocks)
    ]
    for copy in copies:
        copy.start()

    gain = scale[...].astype(F32).reshape(1, width)
    for j in range(0, parts, 2):
        pair = []
        for i in (j, j + 1):
            values = x[i][...].astype(F32).reshape(tokens, width)
            spread = jnp.mean(values * values, axis=-1, keepdims=True)
            pair.append(values * lax.rsqrt(spread + EPS) * gain)
        normed[j * tokens : (j + 2) * tokens, :] = jnp.concatenate(pair, axis=0).astype(BF16)

    low_rank = dot_nt(normed[...], down[...])

    start = pl.multiple_of(index[0] * span, 128)
    mine = normed[:, pl.ds(start, span)]
    pieces = span // HEAD_SIZE
    if heads == 1:
        wide[...] = mine
    else:
        stacked = jnp.concatenate(
            [mine[:, c * HEAD_SIZE : (c + 1) * HEAD_SIZE] for c in range(pieces)], axis=0
        )
        spot = lax.broadcasted_iota(jnp.int32, (HEAD_SIZE, heads * HEAD_SIZE), 1)
        line = lax.broadcasted_iota(jnp.int32, (HEAD_SIZE, heads * HEAD_SIZE), 0)
        for k in range(heads):
            place = jnp.where(spot == line * heads + k, 1.0, 0.0).astype(BF16)
            spread_out = dot(stacked, place).astype(BF16)
            for c in range(pieces):
                wide[
                    k * total : (k + 1) * total,
                    c * heads * HEAD_SIZE : (c + 1) * heads * HEAD_SIZE,
                ] = spread_out[c * total : (c + 1) * total]

    sums = None
    for b in range(blocks):
        copies[b].wait()
        tile = buf[pl.ds(b * chunk, chunk)].reshape(chunk * heads, HEAD_WIDTH)
        part = dot(wide[:, b * chunk * heads : (b + 1) * chunk * heads], tile)
        sums = part if b == 0 else sums + part
    for k in range(heads):
        update = ADAPTER_SCALE * dot_split(low_rank, up[k])
        for j in range(parts):
            here = sums[k * total + j * tokens : k * total + (j + 1) * tokens]
            outs[j][:, k * HEAD_WIDTH : k * HEAD_WIDTH + QUERY_WIDTH] = (
                here[:, :QUERY_WIDTH] + update[j * tokens : (j + 1) * tokens]
            )
            outs[j][:, k * HEAD_WIDTH + QUERY_WIDTH : (k + 1) * HEAD_WIDTH] = here[:, QUERY_WIDTH:]


def attend_kernel(parts, rows, lengths, *refs):
    sums = refs[:parts]
    keys, values, out = refs[parts : parts + 3]
    heads, cache = keys.shape[1:3]
    tokens = out.shape[0]
    projected = sums[0][...]
    for j in range(1, parts):
        projected = projected + sums[j][...]
    lines = GROUP * tokens
    row_of = lax.broadcasted_iota(jnp.int32, (lines, 1), 0) % rows
    position = lax.broadcasted_iota(jnp.int32, (lines, cache), 1)
    limit = jnp.zeros((lines, 1), jnp.int32)
    for r in range(rows):
        limit = jnp.where(row_of == r, lengths[r], limit)
    live = position < limit
    asks = lax.broadcasted_iota(jnp.int32, (lines, tokens), 0) % tokens
    tells = lax.broadcasted_iota(jnp.int32, (lines, tokens), 1)
    seen = (asks % rows == tells % rows) & (tells // rows <= asks // rows)
    scale = 1.0 / HEAD_SIZE**0.5

    def pick(parts_of):
        result = parts_of[0]
        for r in range(1, rows):
            result = jnp.where(row_of == r, parts_of[r], result)
        return result

    for k in range(heads):
        base = k * HEAD_WIDTH
        query = jnp.concatenate(
            [projected[:, base + g * HEAD_SIZE : base + (g + 1) * HEAD_SIZE] for g in range(GROUP)],
            axis=0,
        ).astype(BF16)
        new_keys = projected[:, base + QUERY_WIDTH : base + QUERY_WIDTH + HEAD_SIZE].astype(BF16)
        new_values = projected[:, base + QUERY_WIDTH + HEAD_SIZE : base + HEAD_WIDTH].astype(BF16)
        scores = pick([dot_nt(query, keys[r, k]) for r in range(rows)]) * scale
        scores = jnp.where(live, scores, -1e30)
        window = jnp.where(seen, dot_nt(query, new_keys) * scale, -1e30)
        peak = jnp.maximum(
            jnp.max(scores, axis=-1, keepdims=True), jnp.max(window, axis=-1, keepdims=True)
        )
        exp_cache = jnp.exp(scores - peak)
        exp_window = jnp.exp(window - peak)
        total = jnp.sum(exp_cache, axis=-1, keepdims=True) + jnp.sum(
            exp_window, axis=-1, keepdims=True
        )
        share = 1.0 / total
        weights = (exp_cache * share).astype(BF16)
        weights_window = (exp_window * share).astype(BF16)
        context = pick([dot(weights, values[r, k]) for r in range(rows)])
        context = context + dot(weights_window, new_values)
        for g in range(GROUP):
            first = k * QUERY_WIDTH + g * HEAD_SIZE
            out[:, first : first + HEAD_SIZE] = context[g * tokens : (g + 1) * tokens].astype(BF16)


def output_kernel(parts, blocks, *refs):
    contexts = refs[:parts]
    factors = refs[parts : 2 * parts]
    weight = refs[2 * parts]
    outs = refs[2 * parts + 1 : 3 * parts + 1]
    buf, sems = refs[3 * parts + 1 :]
    depth, width = weight.shape
    tokens = contexts[0].shape[0]
    chunk = depth // blocks
    copies = [
        pltpu.make_async_copy(
            weight.at[pl.ds(b * chunk, chunk)], buf.at[pl.ds(b * chunk, chunk)], sems.at[b]
        )
        for b in range(blocks)
    ]
    for copy in copies:
        copy.start()
    context = jnp.concatenate([c[...].astype(F32) for c in contexts], axis=0).astype(BF16)
    sums = None
    for j in range(parts):
        inner = dot_nt(context, factors[j][:, :depth])
        part = dot_split(inner, factors[j][:, depth:])
        sums = part if j == 0 else sums + part
    sums = ADAPTER_SCALE * sums
    for b in range(blocks):
        copies[b].wait()
        sums = sums + dot(context[:, b * chunk : (b + 1) * chunk], buf[pl.ds(b * chunk, chunk)])
    for j in range(parts):
        outs[j][...] = sums[j * tokens : (j + 1) * tokens].astype(BF16)


def gather_kernel(parts, *refs):
    out = refs[parts]
    width = refs[0].shape[1]
    for j in range(parts):
        out[:, j * width : (j + 1) * width] = refs[j][...]


def finish_kernel(parts, teams, index, x, *refs):
    pieces = refs[:teams]
    out = refs[teams]
    steps, rows, whole = x.shape
    width = whole // parts
    for j in range(parts):
        start = pl.multiple_of((index[0] ^ j) * width, 128)
        attended = pieces[0][:, j * width : (j + 1) * width].astype(F32)
        for t in range(1, teams):
            attended = attended + pieces[t][:, j * width : (j + 1) * width].astype(F32)
        result = x[:, :, pl.ds(start, width)].astype(F32) + attended.reshape(steps, rows, width)
        out[:, :, pl.ds(start, width)] = result.astype(BF16)


def per_device(
    layer_input_rows,
    prenorm_scale,
    query_key_value_weight,
    output_weight,
    query_down_factor,
    query_up_factor,
    output_down_factor,
    output_up_factor,
    stored_keys,
    stored_values,
    lengths,
):
    parts = lax.axis_size("fsdp")
    teams = lax.axis_size("tensor")
    steps, rows, model = layer_input_rows.shape
    tokens = steps * rows
    span, heads = query_key_value_weight.shape[:2]
    ranks = query_down_factor.shape[0]
    index = lax.axis_index("fsdp").astype(jnp.int32).reshape(1)

    x = [layer_input_rows] + [swap(layer_input_rows, "fsdp", j) for j in range(1, parts)]

    factor_width = heads * QUERY_WIDTH + span
    packs = pl.pallas_call(
        functools.partial(pack_kernel, ranks, parts),
        out_shape=[jax.ShapeDtypeStruct((ranks, factor_width), BF16)] * parts,
        in_specs=[SMEM, VMEM, VMEM],
        out_specs=[VMEM] * parts,
        compiler_params=params(16),
        name="pack_factors",
    )(index, output_down_factor, output_up_factor)
    factors = [packs[0]] + [swap(packs[j], "fsdp", j) for j in range(1, parts)]

    blocks = 8
    sums = pl.pallas_call(
        functools.partial(project_kernel, parts, blocks),
        out_shape=[jax.ShapeDtypeStruct((tokens, heads * HEAD_WIDTH), F32)] * parts,
        in_specs=[SMEM] + [VMEM] * parts + [VMEM, ANY, VMEM, VMEM],
        out_specs=[VMEM] * parts,
        scratch_shapes=[
            pltpu.VMEM((parts * tokens, model), BF16),
            pltpu.VMEM((heads * parts * tokens, heads * span), BF16),
            pltpu.VMEM((span, heads, HEAD_WIDTH), BF16),
            pltpu.SemaphoreType.DMA((blocks,)),
        ],
        compiler_params=params(48),
        name="norm_project",
    )(index, *x, prenorm_scale, query_key_value_weight, query_down_factor, query_up_factor)
    sums = [sums[0]] + [swap(sums[j], "fsdp", j) for j in range(1, parts)]

    context = pl.pallas_call(
        functools.partial(attend_kernel, parts, rows),
        out_shape=jax.ShapeDtypeStruct((tokens, heads * QUERY_WIDTH), BF16),
        in_specs=[SMEM] + [VMEM] * parts + [VMEM, VMEM],
        out_specs=VMEM,
        compiler_params=params(32),
        name="attend",
    )(lengths, *sums, stored_keys, stored_values)
    contexts = [context] + [swap(context, "fsdp", j) for j in range(1, parts)]

    partial = pl.pallas_call(
        functools.partial(output_kernel, parts, blocks),
        out_shape=[jax.ShapeDtypeStruct((tokens, span), BF16)] * parts,
        in_specs=[VMEM] * (2 * parts) + [ANY],
        out_specs=[VMEM] * parts,
        scratch_shapes=[
            pltpu.VMEM((heads * QUERY_WIDTH, span), BF16),
            pltpu.SemaphoreType.DMA((blocks,)),
        ],
        compiler_params=params(48),
        name="project_out",
    )(*contexts, *factors, output_weight.reshape(heads * QUERY_WIDTH, span))
    partial = [partial[0]] + [swap(partial[j], "fsdp", j) for j in range(1, parts)]

    gathered = pl.pallas_call(
        functools.partial(gather_kernel, parts),
        out_shape=jax.ShapeDtypeStruct((tokens, model), BF16),
        in_specs=[VMEM] * parts,
        out_specs=VMEM,
        compiler_params=params(16),
        name="gather_columns",
    )(*partial)
    pieces = [gathered] + [swap(gathered, "tensor", j) for j in range(1, teams)]

    return pl.pallas_call(
        functools.partial(finish_kernel, parts, teams),
        out_shape=jax.ShapeDtypeStruct((steps, rows, model), BF16),
        in_specs=[SMEM, VMEM] + [VMEM] * teams,
        out_specs=VMEM,
        compiler_params=params(16),
        name="add_rows",
    )(index, layer_input_rows, *pieces)


def solution(mesh):
    placed = (
        P(None, ("groups", "fsdp"), None),
        P(),
        P("fsdp", "tensor", None),
        P("tensor", None, "fsdp"),
        P("fsdp", None),
        P("tensor", "fsdp", None),
        P("tensor", "fsdp", None),
        P("fsdp", None),
        P(("groups", "fsdp"), "tensor", None, None),
        P(("groups", "fsdp"), "tensor", None, None),
        P(("groups", "fsdp")),
    )
    return jax.shard_map(
        per_device,
        mesh=mesh,
        in_specs=placed,
        out_specs=P(None, ("groups", "fsdp"), None),
        check_vma=False,
    )
```
